256 devices in a mesh: band: 32 (over z_hi, x, y), dom: 8 (over z_lo, core).
Axes of the slice: x: 4, y: 4, z: 8 (z_hi: 2, z_lo: 4; z = z_hi * 4 + z_lo), core: 2. Of those that a mesh axis runs over, the one named last changes fastest.
Arguments:
- states: bfloat16 [256, 48, 24, 128], P('band', 'dom'), may hold values from -8 to 8
- potential: float32 [48, 24, 128], P('dom'), may hold values from -2 to 0
- owners: int32 [2], replicated, may hold values from 0 to 31, as said below
Outputs:
- projected: bfloat16 [256, 48, 24, 128], P('band', 'dom')
The draws below stay inside these ranges and needn't reach their ends.
Inputs may be any that keep to these rules, and one draw needn't show every extreme that they name: `owners`: 2 distinct band indices; the last band index is always among them.
All inputs are finite; a program needn't handle non-finite values.
Results may differ from the reference program's by a relative error of at most 0.0074.
Values may be sent and summed in bfloat16 or wider, within the bound.
No kernel may reach another device: no remote copies, remote signals or barrier semaphores. Data moves between devices by JAX's collectives and lax.ppermute only.
A program may use at most 192 MiB of HBM per device.

```python
import jax
import jax.numpy as jnp
from jax import lax

BLOCK = 8
ROUNDS = 2
NY = 24
NX = 128
NZ = 48
NSTATES = 256
N_BAND = 32


def draw_states(key, part):
    key = jax.random.fold_in(key, 11)
    key_fields, key_mix, key_noise = jax.random.split(key, 3)
    fields = jax.random.normal(key_fields, (8, NZ, NY, NX), jnp.float32)
    mixing = 0.3 * jax.random.normal(key_mix, (NSTATES, 8), jnp.float32)
    total = jnp.zeros((NSTATES, NZ, NY, NX), jnp.float32)
    for member in range(8):
        total = total + mixing[:, member][:, None, None, None] * fields[member][None]
    total = total + 0.5 * jax.random.normal(key_noise, (NSTATES, NZ, NY, NX), jnp.float32)
    return jnp.clip(total, -8.0, 8.0).astype(jnp.bfloat16)


def draw_owners(key, part):
    key = jax.random.fold_in(key, 23)
    key_rest, key_place = jax.random.split(key, 2)
    others = jax.random.permutation(key_rest, N_BAND - 1)[:ROUNDS].astype(jnp.int32)
    others = jnp.concatenate([others, jnp.zeros((ROUNDS,), jnp.int32)])[:ROUNDS]
    place = jax.random.randint(key_place, (), 0, ROUNDS).astype(jnp.int32)
    index = jnp.arange(ROUNDS, dtype=jnp.int32)
    before = others[jnp.clip(index, 0, ROUNDS - 1)]
    after = others[jnp.clip(index - 1, 0, ROUNDS - 1)]
    last = jnp.full((ROUNDS,), N_BAND - 1, jnp.int32)
    return jnp.where(index < place, before, jnp.where(index == place, last, after)).astype(jnp.int32)


def block_levels(key, shape, shards, smallest, largest):
    level, own = 1.0, jax.random.fold_in(key, 6)
    for position, blocks in shards:
        steps = jnp.exp(jax.random.uniform(jax.random.fold_in(own, position), (blocks,), jnp.float32, smallest / len(shards), largest / len(shards)))
        level = level * jnp.repeat(steps, shape[position] // blocks).reshape([-1 if axis == position else 1 for axis in range(len(shape))])
    return level


def setup_inputs(seed: int = 0) -> dict:
    keys = jax.random.split(jax.random.key(seed), 4)
    states = draw_states(jax.random.fold_in(keys[3], 71), 0)
    potential = jnp.clip(-2.0 + 2.0 * jax.random.uniform(keys[1], (NZ, NY, NX), jnp.float32) ** block_levels(keys[1], (NZ, NY, NX), ((0, 8),), -0.2, 0.2), -2.0, 0.0)
    owners = draw_owners(jax.random.fold_in(keys[3], 71), 0)
    return {"states": states, "potential": potential, "owners": owners}


stencil_weights = (-5369.0 / 1800.0, 12.0 / 7.0, -15.0 / 56.0, 10.0 / 189.0, -1.0 / 112.0, 2.0 / 1925.0, -1.0 / 16632.0)
filter_center = 6.0
filter_halfwidth = 5.0


def hamiltonian(values, potential):
    laplace = 3.0 * stencil_weights[0] * values
    for axis_number in (1, 2, 3):
        for offset in range(1, 7):
            laplace = laplace + stencil_weights[offset] * (jnp.roll(values, offset, axis=axis_number) + jnp.roll(values, -offset, axis=axis_number))
    return -0.5 * laplace + potential * values


def filter_block(block, potential):
    center = block.astype(jnp.float32)
    first = ((hamiltonian(center, potential) - filter_center * center) / filter_halfwidth).astype(jnp.bfloat16)
    first_wide = lax.optimization_barrier(first).astype(jnp.float32)
    second = 2.0 * (hamiltonian(first_wide, potential) - filter_center * first_wide) / filter_halfwidth - center
    return second.astype(jnp.bfloat16)


def reference(states, potential, owners):
    grid_shape = states.shape[1:]
    weight = 1.0 / float(NZ * NY * NX)
    blocks = states.reshape((N_BAND, BLOCK) + grid_shape)
    first_raw = lax.dynamic_index_in_dim(blocks, owners[0].astype(jnp.int32), 0, keepdims=False)
    second_raw = lax.dynamic_index_in_dim(blocks, owners[1].astype(jnp.int32), 0, keepdims=False)
    block_zero = filter_block(first_raw, potential).reshape(BLOCK, -1)
    block_one = filter_block(second_raw, potential).reshape(BLOCK, -1)
    block_zero_wide = block_zero.astype(jnp.float32)
    block_one_wide = block_one.astype(jnp.float32)
    contract = (((1,), (1,)), ((), ()))

    def process_block(block):
        filtered = filter_block(block, potential).reshape(BLOCK, -1)
        coef_one = weight * lax.dot_general(block_zero, filtered, contract, preferred_element_type=jnp.float32)
        after_one = filtered.astype(jnp.float32) - jnp.dot(coef_one.T, block_zero_wide, precision=lax.Precision.HIGHEST)
        coef_two = weight * lax.dot_general(block_one_wide, after_one, contract, precision=lax.Precision.HIGHEST)
        result = after_one - jnp.dot(coef_two.T, block_one_wide, precision=lax.Precision.HIGHEST)
        return result.astype(jnp.bfloat16).reshape((BLOCK,) + grid_shape)

    projected = lax.map(process_block, blocks)
    return projected.reshape(states.shape)
```

```python
import functools

import jax
import jax.numpy as jnp
import numpy as np
from jax import lax
from jax.experimental import pallas as pl
from jax.experimental.pallas import tpu as pltpu
from jax.sharding import PartitionSpec as P

ROUNDS = 2
PLANE = 16

stencil_weights = (
    -5369.0 / 1800.0,
    12.0 / 7.0,
    -15.0 / 56.0,
    10.0 / 189.0,
    -1.0 / 112.0,
    2.0 / 1925.0,
    -1.0 / 16632.0,
)
filter_center = 6.0
filter_halfwidth = 5.0
bf16 = jnp.bfloat16
f32 = jnp.float32


def halves(matrix):
    matrix = matrix.astype(np.float32)
    high = matrix.astype(bf16)
    low = (matrix - high.astype(np.float32)).astype(bf16)
    return high, low


def stencil_matrices(planes, ny, nx):
    scale = -0.5 / filter_halfwidth
    rows = planes * ny
    left = np.zeros((rows, 3 * rows), np.float64)
    for p in range(planes):
        for y in range(ny):
            for k in range(1, 7):
                for sign in (k, -k):
                    left[p * ny + y, (planes + p + sign) * ny + y] += scale * stencil_weights[k]
                    left[p * ny + y, (planes + p) * ny + (y + sign) % ny] += scale * stencil_weights[k]
    right = np.zeros((nx, nx), np.float64)
    for x in range(nx):
        for k in range(1, 7):
            for sign in (k, -k):
                right[(x + sign) % nx, x] += scale * stencil_weights[k]
    return np.concatenate(halves(left), axis=0), np.concatenate(halves(right), axis=1)


def apply_filter(before, center, after, potential, left, right):
    count, rows, nx = center.shape
    slabs = [jnp.concatenate([before[s], center[s], after[s]], axis=0) for s in range(count)]
    along_zy = jnp.dot(left, jnp.concatenate(slabs, axis=1), preferred_element_type=f32)
    along_zy = along_zy[:rows] + along_zy[rows:]
    along_x = jnp.dot(center.reshape(count * rows, nx), right, preferred_element_type=f32)
    along_x = (along_x[:, :nx] + along_x[:, nx:]).reshape(count, rows, nx)
    diagonal = (-1.5 * stencil_weights[0] - filter_center) / filter_halfwidth + potential * (1.0 / filter_halfwidth)
    return [
        along_zy[:, s * nx : (s + 1) * nx] + along_x[s] + diagonal * center[s].astype(f32) for s in range(count)
    ]


def first_kernel(before, center, after, potential, left, right, out):
    result = apply_filter(before[...], center[...], after[...], potential[...], left[...], right[...])
    for s, value in enumerate(result):
        out[s] = value.astype(bf16)


def second_kernel(before, center, after, states, potential, left, right, out):
    result = apply_filter(before[...], center[...], after[...], potential[...], left[...], right[...])
    for s, value in enumerate(result):
        out[s] = (2.0 * value - states[s].astype(f32)).astype(bf16)


def select_kernel(owners, pieces, out):
    for turn in range(ROUNDS):
        out[turn] = pieces[lax.rem(owners[turn], PLANE)]


def spread_kernel(owners, place, mine, other, out):
    for turn in range(ROUNDS):
        here = lax.div(owners[turn], PLANE) == place[0]
        value = jnp.where(here, mine[turn], other[turn])
        for target in range(PLANE):
            out[target, turn] = value


def total(value):
    return functools.reduce(lambda a, b: a + b, [value[r : r + 8] for r in range(0, value.shape[0], 8)])


def gram_kernel(gathered, resident, out):
    count, rows, nx = resident.shape
    half = gathered.shape[2]
    out[...] = jnp.zeros_like(out)

    def block(turn, s):
        return jnp.concatenate([gathered[2 * s, turn], gathered[2 * s + 1, turn]], axis=0).astype(f32)

    lines = []
    for turn, other in ((0, None), (1, None), (1, 0)):
        for i in range(count):
            mine = block(turn, i)
            entries = []
            for j in range(count):
                against = resident[j].astype(f32) if other is None else block(other, j)
                entries.append(jnp.sum(total(mine * against), axis=0, keepdims=True))
            lines.append(jnp.concatenate(entries, axis=0))
    for i, line in enumerate(lines):
        out[i] = jnp.sum(line, axis=1, keepdims=True) + jnp.zeros_like(line)


def project_kernel(weight, gram, gathered, resident, out):
    count, rows, nx = resident.shape
    one = [gram[i] * weight for i in range(count)]
    cross = [gram[2 * count + i] for i in range(count)]
    two = []
    for i in range(count):
        value = gram[count + i]
        for k in range(count):
            value = value - cross[i][k : k + 1, :] * one[k]
        two.append(value * weight)
    half = rows // 2
    for part in range(2):
        for j in range(count):
            value = resident[j].astype(f32)[part * half : (part + 1) * half]
            for i in range(count):
                value = value - one[i][j : j + 1] * gathered[2 * i + part, 0].astype(f32)
            for i in range(count):
                value = value - two[i][j : j + 1] * gathered[2 * i + part, 1].astype(f32)
            out[j, part * half : (part + 1) * half] = value.astype(bf16)


vmem = pl.BlockSpec(memory_space=pltpu.VMEM)
smem = pl.BlockSpec(memory_space=pltpu.SMEM)
params = pltpu.CompilerParams(vmem_limit_bytes=48 * 1024 * 1024)


def call(kernel, shape, dtype, specs, *operands, name):
    return pl.pallas_call(
        kernel,
        out_shape=jax.ShapeDtypeStruct(shape, dtype),
        in_specs=specs,
        out_specs=vmem,
        compiler_params=params,
        name=name,
    )(*operands)


def neighbours(cells):
    count = lax.axis_size("dom")
    ahead = [(i, (i + 1) % count) for i in range(count)]
    return lax.ppermute(cells, "dom", ahead), lax.ppermute(cells, "dom", [(b, a) for a, b in ahead])


def on_device(states, potential, owners):
    count, planes, ny, nx = states.shape
    rows = planes * ny
    weight = 1.0 / float(planes * lax.axis_size("dom") * ny * nx)
    bands = lax.axis_size("band")
    groups = [list(range(start, start + PLANE)) for start in range(0, bands, PLANE)]
    place = (lax.axis_index("band") // PLANE).astype(jnp.int32).reshape(1)
    left, right = stencil_matrices(planes, ny, nx)
    left, right = jnp.asarray(left), jnp.asarray(right)
    states = states.reshape(count, rows, nx)
    potential = potential.reshape(rows, nx)

    before, after = neighbours(states)
    first = call(
        first_kernel, states.shape, bf16, [vmem] * 6, before, states, after, potential, left, right, name="first"
    )
    before, after = neighbours(first)
    resident = call(
        second_kernel, states.shape, bf16, [vmem] * 7, before, first, after, states, potential, left, right,
        name="second",
    )
    half = count * rows // PLANE
    pieces = lax.all_to_all(resident.reshape(PLANE, half, nx), "band", 0, 0, axis_index_groups=groups)
    mine = call(select_kernel, (ROUNDS, half, nx), bf16, [smem, vmem], owners, pieces, name="select")
    other = lax.ppermute(mine, "band", [(i, (i + PLANE) % bands) for i in range(bands)])
    copies = call(
        spread_kernel, (PLANE, ROUNDS, half, nx), bf16, [smem, smem, vmem, vmem], owners, place, mine, other,
        name="spread",
    )
    gathered = lax.all_to_all(copies, "band", 0, 0, axis_index_groups=groups)
    gram = call(gram_kernel, (3 * count, count, nx), f32, [vmem, vmem], gathered, resident, name="gram")
    gram = lax.psum(gram[:, :, 0], "dom")
    gram = jnp.broadcast_to(gram[:, :, None], (3 * count, count, nx))
    result = call(
        functools.partial(project_kernel, weight), states.shape, bf16, [vmem] * 3, gram, gathered, resident,
        name="project",
    )
    return result.reshape(count, planes, ny, nx)


def solution(mesh):
    return jax.shard_map(
        on_device,
        mesh=mesh,
        in_specs=(P("band", "dom", None, None), P("dom", None, None), P()),
        out_specs=P("band", "dom", None, None),
        check_vma=False,
    )
```

```python
import functools

import jax
import jax.numpy as jnp
import numpy as np
from jax import lax
from jax.experimental import pallas as pl
from jax.experimental.pallas import tpu as pltpu
from jax.sharding import PartitionSpec as P

ROUNDS = 2
PLANE = 16
GROUP = 8

stencil_weights = (
    -5369.0 / 1800.0,
    12.0 / 7.0,
    -15.0 / 56.0,
    10.0 / 189.0,
    -1.0 / 112.0,
    2.0 / 1925.0,
    -1.0 / 16632.0,
)
filter_center = 6.0
filter_halfwidth = 5.0
bf16 = jnp.bfloat16
f32 = jnp.float32


def halves(matrix):
    matrix = matrix.astype(np.float32)
    high = matrix.astype(bf16)
    low = (matrix - high.astype(np.float32)).astype(bf16)
    return high, low


def stencil_matrices(planes, ny, nx):
    scale = -0.5 / filter_halfwidth
    rows = planes * ny
    left = np.zeros((rows, 3 * rows), np.float64)
    for p in range(planes):
        for y in range(ny):
            for k in range(1, 7):
                for sign in (k, -k):
                    left[p * ny + y, (planes + p + sign) * ny + y] += scale * stencil_weights[k]
                    left[p * ny + y, (planes + p) * ny + (y + sign) % ny] += scale * stencil_weights[k]
    along_x = np.zeros((nx, nx), np.float64)
    for x in range(nx):
        for k in range(1, 7):
            for sign in (k, -k):
                along_x[(x + sign) % nx, x] += scale * stencil_weights[k]
    inside = np.concatenate(halves(left[:, rows : 2 * rows]), axis=0)
    beside = np.concatenate(halves(np.concatenate([left[:, :rows], left[:, 2 * rows :]], axis=1)), axis=0)
    return tuple(jnp.asarray(m) for m in (inside, beside, np.concatenate(halves(along_x), axis=1)))


def diagonal_of(potential):
    return (-1.5 * stencil_weights[0] - filter_center) / filter_halfwidth + potential * (1.0 / filter_halfwidth)


def inner_part(center, diagonals, inside, along_x):
    count, rows, nx = center.shape
    zy = jnp.dot(inside, jnp.concatenate([center[s] for s in range(count)], axis=1), preferred_element_type=f32)
    zy = zy[:rows] + zy[rows:]
    x = jnp.dot(center.reshape(count * rows, nx), along_x, preferred_element_type=f32)
    x = (x[:, :nx] + x[:, nx:]).reshape(count, rows, nx)
    return [zy[:, s * nx : (s + 1) * nx] + x[s] + diagonals[s] * center[s].astype(f32) for s in range(count)]


def outer_part(before, after, beside):
    count, rows, nx = before.shape
    slabs = [jnp.concatenate([before[s], after[s]], axis=0) for s in range(count)]
    zy = jnp.dot(beside, jnp.concatenate(slabs, axis=1), preferred_element_type=f32)
    zy = zy[:rows] + zy[rows:]
    return [zy[:, s * nx : (s + 1) * nx] for s in range(count)]


def inner_kernel(center, potential, inside, along_x, out):
    for s, value in enumerate(inner_part(center[...], [diagonal_of(potential[...])] * center.shape[0], inside[...], along_x[...])):
        out[s] = value


def first_kernel(before, after, inner, beside, out):
    for s, value in enumerate(outer_part(before[...], after[...], beside[...])):
        out[s] = (inner[s] + value).astype(bf16)


def second_kernel(before, after, inner, states, beside, out):
    for s, value in enumerate(outer_part(before[...], after[...], beside[...])):
        out[s] = (2.0 * (inner[s] + value) - states[s].astype(f32)).astype(bf16)


def owner_kernel(slab_a, slab_b, slab_c, slab_d, slab_e, pot_b, pot_c, pot_d, inside, beside, along_x, out):
    inside, beside, along_x = inside[...], beside[...], along_x[...]
    middle = jnp.stack([slab_b[...], slab_c[...], slab_d[...]])
    first = []
    before = jnp.stack([slab_a[...], slab_b[...], slab_c[...]])
    after = jnp.stack([slab_c[...], slab_d[...], slab_e[...]])
    outer = outer_part(before, after, beside)
    diagonals = [diagonal_of(p[...]) for p in (pot_b, pot_c, pot_d)]
    inner = inner_part(middle, diagonals, inside, along_x)
    first = [(i + o).astype(bf16)[None] for i, o in zip(inner, outer)]
    value = inner_part(first[1], diagonals[1:2], inside, along_x)[0] + outer_part(first[0], first[2], beside)[0]
    block = (2.0 * value - slab_c[...].astype(f32)).astype(bf16)
    for target in range(PLANE):
        out[target] = block


def by_rows(blocks):
    return jnp.concatenate(
        [jnp.concatenate([b[r : r + GROUP] for r in range(0, b.shape[0], GROUP)], axis=1) for b in blocks], axis=0
    ).astype(bf16)


def same_row(shape):
    row = lax.broadcasted_iota(jnp.int32, shape, 0) % GROUP
    return row == lax.broadcasted_iota(jnp.int32, shape, 1) % GROUP


def gram_kernel(gathered, resident, out, rows_out):
    count = resident.shape[0]
    blocks = []
    for turn in range(ROUNDS):
        for s in range(count):
            blocks.append(gathered[turn * count + s].astype(f32))
    owned = by_rows(blocks)
    against = jnp.concatenate(
        [by_rows([resident[j].astype(f32) for j in range(count)]), owned[: count * GROUP]], axis=0
    )
    products = lax.dot_general(owned, against, (((1,), (1,)), ((), ())), preferred_element_type=f32)
    products = jnp.where(same_row(products.shape), products, 0.0)
    out[...] = jnp.sum(products.reshape(ROUNDS * count, GROUP, products.shape[1]), axis=1)
    rows_out[...] = owned


def project_kernel(weight, gram, owned, resident, out):
    count, rows, nx = resident.shape
    lanes = gram.shape[1]
    group = lax.broadcasted_iota(jnp.int32, (lanes, lanes), 0) // GROUP
    same_group = jnp.where(group == lax.broadcasted_iota(jnp.int32, (lanes, lanes), 1) // GROUP, 1.0, 0.0)
    sums = jnp.dot(gram[...], same_group, precision=lax.Precision.HIGHEST, preferred_element_type=f32)
    one = sums[:count] * weight
    two = sums[count:]
    for k in range(count):
        lane = (count + k) * GROUP
        two = two - sums[count:, lane : lane + 1] * one[k : k + 1]
    coef = jnp.concatenate([one, two * weight], axis=0)
    spread = jnp.broadcast_to(coef[:, None, :], (ROUNDS * count, GROUP, lanes)).reshape(lanes, lanes)
    spread = jnp.where(same_row(spread.shape), spread, 0.0).T[: count * GROUP]
    high = spread.astype(bf16)
    low = (spread - high.astype(f32)).astype(bf16)
    taken = jnp.dot(jnp.concatenate([high, low], axis=0), owned[...], preferred_element_type=f32)
    taken = taken[: count * GROUP] + taken[count * GROUP :]
    for j in range(count):
        mine = taken[j * GROUP : (j + 1) * GROUP]
        mine = jnp.concatenate([mine[:, b * nx : (b + 1) * nx] for b in range(rows // GROUP)], axis=0)
        out[j] = (resident[j].astype(f32) - mine).astype(bf16)


vmem = pl.BlockSpec(memory_space=pltpu.VMEM)
smem = pl.BlockSpec(memory_space=pltpu.SMEM)
params = pltpu.CompilerParams(vmem_limit_bytes=40 * 1024 * 1024)


def call(kernel, out_shape, specs, *operands, name):
    return pl.pallas_call(
        kernel,
        out_shape=out_shape,
        in_specs=specs,
        out_specs=jax.tree.map(lambda _: vmem, out_shape),
        compiler_params=params,
        name=name,
    )(*operands)


def on_device(states, potential, owners):
    count, planes, ny, nx = states.shape
    rows = planes * ny
    doms, bands = lax.axis_size("dom"), lax.axis_size("band")
    weight = 1.0 / float(planes * doms * ny * nx)
    band = lax.axis_index("band")
    inside, beside, along_x = stencil_matrices(planes, ny, nx)
    states = states.reshape(count, rows, nx)
    potential = potential.reshape(rows, nx)
    block = jax.ShapeDtypeStruct(states.shape, bf16)
    wide = jax.ShapeDtypeStruct(states.shape, f32)
    cells = (rows, nx)
    groups = [list(range(start, start + PLANE)) for start in range(0, bands, PLANE)]

    def both_ways(values):
        ring = [(i, (i + 1) % doms) for i in range(doms)]
        return lax.ppermute(values, "dom", ring), lax.ppermute(values, "dom", [(b, a) for a, b in ring])

    def along_z(values, step):
        pairs = []
        for b in range(bands):
            for d in range(doms):
                place = (b // PLANE * doms + d + step) % (bands // PLANE * doms)
                pairs.append((b * doms + d, (place // doms * PLANE + b % PLANE) * doms + place % doms))
        return lax.ppermute(values, ("band", "dom"), pairs)

    owner = lax.dynamic_index_in_dim(owners, band % PLANE // count, 0, keepdims=False)
    twice = jnp.broadcast_to(states[None], (ROUNDS,) + states.shape).reshape((PLANE,) + cells)
    pieces = lax.all_to_all(twice, "band", 0, 0, axis_index_groups=groups)
    before, after = both_ways(states)
    inner = call(inner_kernel, wide, [vmem] * 4, states, potential, inside, along_x, name="first_inner")
    first = call(first_kernel, block, [vmem] * 4, before, after, inner, beside, name="first")
    pieces, first = lax.optimization_barrier((pieces, first))
    mine = lax.dynamic_index_in_dim(pieces, owner % PLANE, 0, keepdims=False)
    mine = jnp.where(owner // PLANE == band // PLANE, mine, jnp.zeros_like(mine))
    raw = mine + lax.ppermute(mine, "band", [(i, (i + PLANE) % bands) for i in range(bands)])
    near = [along_z(raw, step) for step in (1, -1, 2, -2)]
    pot_before, pot_after = along_z(potential, 1), along_z(potential, -1)

    before, after = both_ways(first)
    inner = call(inner_kernel, wide, [vmem] * 4, first, potential, inside, along_x, name="second_inner")
    resident = call(second_kernel, block, [vmem] * 5, before, after, inner, states, beside, name="second")

    copies = call(
        owner_kernel, jax.ShapeDtypeStruct((PLANE,) + cells, bf16), [vmem] * 11,
        near[2], near[0], raw, near[1], near[3], pot_before, potential, pot_after, inside, beside, along_x,
        name="owner",
    )
    gathered = lax.all_to_all(copies, "band", 0, 0, axis_index_groups=groups)
    gram, owned = call(
        gram_kernel,
        (
            jax.ShapeDtypeStruct((ROUNDS * count, ROUNDS * count * GROUP), f32),
            jax.ShapeDtypeStruct((ROUNDS * count * GROUP, rows // GROUP * nx), bf16),
        ),
        [vmem] * 2, gathered, resident, name="gram",
    )
    gram = gram + lax.ppermute(gram, "dom", [(i, i ^ 1) for i in range(doms)])
    gram = gram + sum(lax.ppermute(gram, "dom", [(i, i ^ s) for i in range(doms)]) for s in range(2, doms, 2))
    result = call(
        functools.partial(project_kernel, weight), block, [vmem] * 3, gram, owned, resident, name="project"
    )
    return result.reshape(count, planes, ny, nx)


def solution(mesh):
    return jax.shard_map(
        on_device,
        mesh=mesh,
        in_specs=(P("band", "dom", None, None), P("dom", None, None), P()),
        out_specs=P("band", "dom", None, None),
        check_vma=False,
    )
```

```python
import functools

import jax
import jax.numpy as jnp
import numpy as np
from jax import lax
from jax.experimental import pallas as pl
from jax.experimental.pallas import tpu as pltpu
from jax.sharding import PartitionSpec as P

ROUNDS = 2
PLANE = 16
GROUP = 8

stencil_weights = (
    -5369.0 / 1800.0,
    12.0 / 7.0,
    -15.0 / 56.0,
    10.0 / 189.0,
    -1.0 / 112.0,
    2.0 / 1925.0,
    -1.0 / 16632.0,
)
filter_center = 6.0
filter_halfwidth = 5.0
bf16 = jnp.bfloat16
f32 = jnp.float32


def halves(matrix):
    matrix = matrix.astype(np.float32)
    high = matrix.astype(bf16)
    low = (matrix - high.astype(np.float32)).astype(bf16)
    return high, low


def stencil_matrices(planes, ny, nx):
    scale = -0.5 / filter_halfwidth
    rows = planes * ny
    left = np.zeros((rows, 3 * rows), np.float64)
    for p in range(planes):
        for y in range(ny):
            for k in range(1, 7):
                for sign in (k, -k):
                    left[p * ny + y, (planes + p + sign) * ny + y] += scale * stencil_weights[k]
                    left[p * ny + y, (planes + p) * ny + (y + sign) % ny] += scale * stencil_weights[k]
    along_x = np.zeros((nx, nx), np.float64)
    for x in range(nx):
        for k in range(1, 7):
            for sign in (k, -k):
                along_x[(x + sign) % nx, x] += scale * stencil_weights[k]
    inside = np.concatenate(halves(left[:, rows : 2 * rows]), axis=0)
    beside = np.concatenate(halves(np.concatenate([left[:, :rows], left[:, 2 * rows :]], axis=1)), axis=0)
    return tuple(jnp.asarray(m) for m in (inside, beside, np.concatenate(halves(along_x), axis=1)))


def diagonal_of(potential):
    return (-1.5 * stencil_weights[0] - filter_center) / filter_halfwidth + potential * (1.0 / filter_halfwidth)


def inner_part(center, diagonals, inside, along_x):
    count, rows, nx = center.shape
    zy = jnp.dot(inside, jnp.concatenate([center[s] for s in range(count)], axis=1), preferred_element_type=f32)
    zy = zy[:rows] + zy[rows:]
    x = jnp.dot(center.reshape(count * rows, nx), along_x, preferred_element_type=f32)
    x = (x[:, :nx] + x[:, nx:]).reshape(count, rows, nx)
    return [zy[:, s * nx : (s + 1) * nx] + x[s] + diagonals[s] * center[s].astype(f32) for s in range(count)]


def outer_part(before, after, beside):
    count, rows, nx = before.shape
    slabs = [jnp.concatenate([before[s], after[s]], axis=0) for s in range(count)]
    zy = jnp.dot(beside, jnp.concatenate(slabs, axis=1), preferred_element_type=f32)
    zy = zy[:rows] + zy[rows:]
    return [zy[:, s * nx : (s + 1) * nx] for s in range(count)]


def twice_kernel(states, out, done):
    count = states.shape[0]
    copies = [pltpu.make_async_copy(states, out.at[pl.ds(k * count, count)], done.at[k]) for k in range(ROUNDS)]
    for copy in copies:
        copy.start()
    for copy in copies:
        copy.wait()


def inner_kernel(center, potential, inside, along_x, out):
    for s, value in enumerate(inner_part(center[...], [diagonal_of(potential[...])] * center.shape[0], inside[...], along_x[...])):
        out[s] = value


def first_kernel(before, after, inner, beside, out):
    for s, value in enumerate(outer_part(before[...], after[...], beside[...])):
        out[s] = (inner[s] + value).astype(bf16)


def second_kernel(before, after, inner, states, beside, out):
    for s, value in enumerate(outer_part(before[...], after[...], beside[...])):
        out[s] = (2.0 * (inner[s] + value) - states[s].astype(f32)).astype(bf16)


def owner_kernel(slab_a, slab_b, slab_c, slab_d, slab_e, pot_b, pot_c, pot_d, inside, beside, along_x, out):
    inside, beside, along_x = inside[...], beside[...], along_x[...]
    middle = jnp.stack([slab_b[...], slab_c[...], slab_d[...]])
    first = []
    before = jnp.stack([slab_a[...], slab_b[...], slab_c[...]])
    after = jnp.stack([slab_c[...], slab_d[...], slab_e[...]])
    outer = outer_part(before, after, beside)
    diagonals = [diagonal_of(p[...]) for p in (pot_b, pot_c, pot_d)]
    inner = inner_part(middle, diagonals, inside, along_x)
    first = [(i + o).astype(bf16)[None] for i, o in zip(inner, outer)]
    value = inner_part(first[1], diagonals[1:2], inside, along_x)[0] + outer_part(first[0], first[2], beside)[0]
    block = (2.0 * value - slab_c[...].astype(f32)).astype(bf16)
    for target in range(PLANE):
        out[target] = block


def by_rows(blocks):
    return jnp.concatenate(
        [jnp.concatenate([b[r : r + GROUP] for r in range(0, b.shape[0], GROUP)], axis=1) for b in blocks], axis=0
    ).astype(bf16)


def same_row(shape):
    row = lax.broadcasted_iota(jnp.int32, shape, 0) % GROUP
    return row == lax.broadcasted_iota(jnp.int32, shape, 1) % GROUP


def gram_kernel(gathered, resident, out, rows_out):
    count = resident.shape[0]
    blocks = []
    for turn in range(ROUNDS):
        for s in range(count):
            blocks.append(gathered[turn * count + s].astype(f32))
    owned = by_rows(blocks)
    against = jnp.concatenate(
        [by_rows([resident[j].astype(f32) for j in range(count)]), owned[: count * GROUP]], axis=0
    )
    products = lax.dot_general(owned, against, (((1,), (1,)), ((), ())), preferred_element_type=f32)
    products = jnp.where(same_row(products.shape), products, 0.0)
    out[...] = jnp.sum(products.reshape(ROUNDS * count, GROUP, products.shape[1]), axis=1)
    rows_out[...] = owned


def project_kernel(weight, gram, owned, resident, out):
    count, rows, nx = resident.shape
    lanes = gram.shape[1]
    group = lax.broadcasted_iota(jnp.int32, (lanes, lanes), 0) // GROUP
    same_group = jnp.where(group == lax.broadcasted_iota(jnp.int32, (lanes, lanes), 1) // GROUP, 1.0, 0.0)
    sums = jnp.dot(gram[...], same_group, precision=lax.Precision.HIGHEST, preferred_element_type=f32)
    one = sums[:count] * weight
    two = sums[count:]
    for k in range(count):
        lane = (count + k) * GROUP
        two = two - sums[count:, lane : lane + 1] * one[k : k + 1]
    coef = jnp.concatenate([one, two * weight], axis=0)
    spread = jnp.broadcast_to(coef[:, None, :], (ROUNDS * count, GROUP, lanes)).reshape(lanes, lanes)
    spread = jnp.where(same_row(spread.shape), spread, 0.0).T[: count * GROUP]
    high = spread.astype(bf16)
    low = (spread - high.astype(f32)).astype(bf16)
    taken = jnp.dot(jnp.concatenate([high, low], axis=0), owned[...], preferred_element_type=f32)
    taken = taken[: count * GROUP] + taken[count * GROUP :]
    for j in range(count):
        mine = taken[j * GROUP : (j + 1) * GROUP]
        mine = jnp.concatenate([mine[:, b * nx : (b + 1) * nx] for b in range(rows // GROUP)], axis=0)
        out[j] = (resident[j].astype(f32) - mine).astype(bf16)


vmem = pl.BlockSpec(memory_space=pltpu.VMEM)
smem = pl.BlockSpec(memory_space=pltpu.SMEM)
params = pltpu.CompilerParams(vmem_limit_bytes=40 * 1024 * 1024)


def call(kernel, out_shape, specs, *operands, name):
    return pl.pallas_call(
        kernel,
        out_shape=out_shape,
        in_specs=specs,
        out_specs=jax.tree.map(lambda _: vmem, out_shape),
        compiler_params=params,
        name=name,
    )(*operands)


def on_device(states, potential, owners):
    count, planes, ny, nx = states.shape
    rows = planes * ny
    doms, bands = lax.axis_size("dom"), lax.axis_size("band")
    weight = 1.0 / float(planes * doms * ny * nx)
    band = lax.axis_index("band")
    inside, beside, along_x = stencil_matrices(planes, ny, nx)
    states = states.reshape(count, rows, nx)
    potential = potential.reshape(rows, nx)
    block = jax.ShapeDtypeStruct(states.shape, bf16)
    wide = jax.ShapeDtypeStruct(states.shape, f32)
    cells = (rows, nx)
    groups = [list(range(start, start + PLANE)) for start in range(0, bands, PLANE)]

    def both_ways(values):
        ring = [(i, (i + 1) % doms) for i in range(doms)]
        return lax.ppermute(values, "dom", ring), lax.ppermute(values, "dom", [(b, a) for a, b in ring])

    def along_z(values, step):
        pairs = []
        for b in range(bands):
            for d in range(doms):
                place = (b // PLANE * doms + d + step) % (bands // PLANE * doms)
                pairs.append((b * doms + d, (place // doms * PLANE + b % PLANE) * doms + place % doms))
        return lax.ppermute(values, ("band", "dom"), pairs)

    hbm = pl.BlockSpec(memory_space=pltpu.HBM)
    twice = pl.pallas_call(
        twice_kernel,
        out_shape=jax.ShapeDtypeStruct((ROUNDS * count,) + cells, bf16),
        in_specs=[hbm],
        out_specs=hbm,
        scratch_shapes=[pltpu.SemaphoreType.DMA((ROUNDS,))],
        compiler_params=params,
        name="twice",
    )(states)
    pieces = lax.all_to_all(twice, "band", 0, 0, axis_index_groups=groups)
    before, after = both_ways(states)
    inner = call(inner_kernel, wide, [vmem] * 4, states, potential, inside, along_x, name="first_inner")
    owner = jnp.where((band >> 3) & 1 == 0, owners[0], owners[1])
    mine = lax.dynamic_index_in_dim(pieces, owner & (PLANE - 1), 0, keepdims=False)
    mine = jnp.where(owner >> 4 == band >> 4, mine, jnp.zeros_like(mine))
    other = lax.ppermute(mine, "band", [(i, (i + PLANE) % bands) for i in range(bands)])
    first = call(first_kernel, block, [vmem] * 4, before, after, inner, beside, name="first")
    other, first = lax.optimization_barrier((other, first))
    raw = mine + other
    near = [along_z(raw, step) for step in (1, -1, 2, -2)]
    pot_before, pot_after = along_z(potential, 1), along_z(potential, -1)

    before, after = both_ways(first)
    inner = call(inner_kernel, wide, [vmem] * 4, first, potential, inside, along_x, name="second_inner")
    resident = call(second_kernel, block, [vmem] * 5, before, after, inner, states, beside, name="second")

    copies = call(
        owner_kernel, jax.ShapeDtypeStruct((PLANE,) + cells, bf16), [vmem] * 11,
        near[2], near[0], raw, near[1], near[3], pot_before, potential, pot_after, inside, beside, along_x,
        name="owner",
    )
    gathered = lax.all_to_all(copies, "band", 0, 0, axis_index_groups=groups)
    gram, owned = call(
        gram_kernel,
        (
            jax.ShapeDtypeStruct((ROUNDS * count, ROUNDS * count * GROUP), f32),
            jax.ShapeDtypeStruct((ROUNDS * count * GROUP, rows // GROUP * nx), bf16),
        ),
        [vmem] * 2, gathered, resident, name="gram",
    )
    gram = gram + lax.ppermute(gram, "dom", [(i, i ^ 1) for i in range(doms)])
    gram = gram + sum(lax.ppermute(gram, "dom", [(i, i ^ s) for i in range(doms)]) for s in range(2, doms, 2))
    result = call(
        functools.partial(project_kernel, weight), block, [vmem] * 3, gram, owned, resident, name="project"
    )
    return result.reshape(count, planes, ny, nx)


def solution(mesh):
    return jax.shard_map(
        on_device,
        mesh=mesh,
        in_specs=(P("band", "dom", None, None), P("dom", None, None), P()),
        out_specs=P("band", "dom", None, None),
        check_vma=False,
    )
```

```python
import functools

import jax
import jax.numpy as jnp
import numpy as np
from jax import lax
from jax.experimental import pallas as pl
from jax.experimental.pallas import tpu as pltpu
from jax.sharding import PartitionSpec as P

ROUNDS = 2
PLANE = 16
GROUP = 8

stencil_weights = (
    -5369.0 / 1800.0,
    12.0 / 7.0,
    -15.0 / 56.0,
    10.0 / 189.0,
    -1.0 / 112.0,
    2.0 / 1925.0,
    -1.0 / 16632.0,
)
filter_center = 6.0
filter_halfwidth = 5.0
bf16 = jnp.bfloat16
f32 = jnp.float32


def halves(matrix):
    matrix = matrix.astype(np.float32)
    high = matrix.astype(bf16)
    low = (matrix - high.astype(np.float32)).astype(bf16)
    return high, low


def stencil_matrices(planes, ny, nx):
    scale = -0.5 / filter_halfwidth
    rows = planes * ny
    left = np.zeros((rows, 3 * rows), np.float64)
    for p in range(planes):
        for y in range(ny):
            for k in range(1, 7):
                for sign in (k, -k):
                    left[p * ny + y, (planes + p + sign) * ny + y] += scale * stencil_weights[k]
                    left[p * ny + y, (planes + p) * ny + (y + sign) % ny] += scale * stencil_weights[k]
    along_x = np.zeros((nx, nx), np.float64)
    for x in range(nx):
        for k in range(1, 7):
            for sign in (k, -k):
                along_x[(x + sign) % nx, x] += scale * stencil_weights[k]
    inside = np.concatenate(halves(left[:, rows : 2 * rows]), axis=0)
    beside = np.concatenate(halves(np.concatenate([left[:, :rows], left[:, 2 * rows :]], axis=1)), axis=0)
    return tuple(jnp.asarray(m) for m in (inside, beside, np.concatenate(halves(along_x), axis=1)))


def diagonal_of(potential):
    return (-1.5 * stencil_weights[0] - filter_center) / filter_halfwidth + potential * (1.0 / filter_halfwidth)


def inner_part(center, diagonals, inside, along_x):
    count, rows, nx = center.shape
    zy = jnp.dot(inside, jnp.concatenate([center[s] for s in range(count)], axis=1), preferred_element_type=f32)
    zy = zy[:rows] + zy[rows:]
    x = jnp.dot(center.reshape(count * rows, nx), along_x, preferred_element_type=f32)
    x = (x[:, :nx] + x[:, nx:]).reshape(count, rows, nx)
    return [zy[:, s * nx : (s + 1) * nx] + x[s] + diagonals[s] * center[s].astype(f32) for s in range(count)]


def outer_part(before, after, beside):
    count, rows, nx = before.shape
    slabs = [jnp.concatenate([before[s], after[s]], axis=0) for s in range(count)]
    zy = jnp.dot(beside, jnp.concatenate(slabs, axis=1), preferred_element_type=f32)
    zy = zy[:rows] + zy[rows:]
    return [zy[:, s * nx : (s + 1) * nx] for s in range(count)]


def twice_kernel(states, out, done):
    count = states.shape[0]
    copies = [pltpu.make_async_copy(states, out.at[pl.ds(k * count, count)], done.at[k]) for k in range(ROUNDS)]
    for copy in copies:
        copy.start()
    for copy in copies:
        copy.wait()


def first_inner_kernel(center, potential, inside, along_x, out, diagonal_out, terms_out):
    diagonal = diagonal_of(potential[...])
    diagonal_out[...] = diagonal
    high = potential[...].astype(bf16)
    terms_out[0] = high
    terms_out[1] = (potential[...] - high.astype(f32)).astype(bf16)
    for s, value in enumerate(inner_part(center[...], [diagonal] * center.shape[0], inside[...], along_x[...])):
        out[s] = value


def second_inner_kernel(center, diagonal, inside, along_x, out):
    for s, value in enumerate(inner_part(center[...], [diagonal[...]] * center.shape[0], inside[...], along_x[...])):
        out[s] = value


def first_kernel(before, after, inner, beside, out):
    for s, value in enumerate(outer_part(before[...], after[...], beside[...])):
        out[s] = (inner[s] + value).astype(bf16)


def second_kernel(before, after, inner, states, beside, out):
    for s, value in enumerate(outer_part(before[...], after[...], beside[...])):
        out[s] = (2.0 * (inner[s] + value) - states[s].astype(f32)).astype(bf16)


def owner_kernel(slab_a, near_b, slab_c, near_d, slab_e, diagonal, inside, beside, along_x, out):
    inside, beside, along_x = inside[...], beside[...], along_x[...]
    middle = jnp.stack([near_b[0], slab_c[...], near_d[0]])
    before = jnp.stack([slab_a[...], near_b[0], slab_c[...]])
    after = jnp.stack([slab_c[...], near_d[0], slab_e[...]])
    outer = outer_part(before, after, beside)
    beside_diagonals = [diagonal_of(n[1].astype(f32) + n[2].astype(f32)) for n in (near_b, near_d)]
    diagonals = [beside_diagonals[0], diagonal[...], beside_diagonals[1]]
    inner = inner_part(middle, diagonals, inside, along_x)
    first = [(i + o).astype(bf16)[None] for i, o in zip(inner, outer)]
    value = inner_part(first[1], diagonals[1:2], inside, along_x)[0] + outer_part(first[0], first[2], beside)[0]
    block = (2.0 * value - slab_c[...].astype(f32)).astype(bf16)
    for target in range(PLANE):
        out[target] = block


def by_rows(blocks):
    return jnp.concatenate(
        [jnp.concatenate([b[r : r + GROUP] for r in range(0, b.shape[0], GROUP)], axis=1) for b in blocks], axis=0
    ).astype(bf16)


def same_row(shape):
    row = lax.broadcasted_iota(jnp.int32, shape, 0) % GROUP
    return row == lax.broadcasted_iota(jnp.int32, shape, 1) % GROUP


def gram_kernel(gathered, resident, out, rows_out):
    count = resident.shape[0]
    blocks = []
    for turn in range(ROUNDS):
        for s in range(count):
            blocks.append(gathered[turn * count + s].astype(f32))
    owned = by_rows(blocks)
    against = jnp.concatenate(
        [by_rows([resident[j].astype(f32) for j in range(count)]), owned[: count * GROUP]], axis=0
    )
    products = lax.dot_general(owned, against, (((1,), (1,)), ((), ())), preferred_element_type=f32)
    products = jnp.where(same_row(products.shape), products, 0.0)
    out[...] = jnp.sum(products.reshape(ROUNDS * count, GROUP, products.shape[1]), axis=1)
    rows_out[...] = owned


def project_kernel(weight, gram, owned, resident, out):
    count, rows, nx = resident.shape
    lanes = gram.shape[1]
    group = lax.broadcasted_iota(jnp.int32, (lanes, lanes), 0) // GROUP
    same_group = jnp.where(group == lax.broadcasted_iota(jnp.int32, (lanes, lanes), 1) // GROUP, 1.0, 0.0)
    left, terms = gram[...], []
    for _ in range(3):
        terms.append(left.astype(bf16))
        left = left - terms[-1].astype(f32)
    sums = jnp.dot(jnp.concatenate(terms, axis=0), same_group.astype(bf16), preferred_element_type=f32)
    sums = sums[: 2 * count] + (sums[2 * count : 4 * count] + sums[4 * count :])
    one = sums[:count] * weight
    two = sums[count:]
    for k in range(count):
        lane = (count + k) * GROUP
        two = two - sums[count:, lane : lane + 1] * one[k : k + 1]
    coef = jnp.concatenate([one, two * weight], axis=0)
    spread = jnp.broadcast_to(coef[:, None, :], (ROUNDS * count, GROUP, lanes)).reshape(lanes, lanes)
    spread = jnp.where(same_row(spread.shape), spread, 0.0).T[: count * GROUP]
    high = spread.astype(bf16)
    low = (spread - high.astype(f32)).astype(bf16)
    taken = jnp.dot(jnp.concatenate([high, low], axis=0), owned[...], preferred_element_type=f32)
    taken = taken[: count * GROUP] + taken[count * GROUP :]
    for j in range(count):
        mine = taken[j * GROUP : (j + 1) * GROUP]
        mine = jnp.concatenate([mine[:, b * nx : (b + 1) * nx] for b in range(rows // GROUP)], axis=0)
        out[j] = (resident[j].astype(f32) - mine).astype(bf16)


vmem = pl.BlockSpec(memory_space=pltpu.VMEM)
smem = pl.BlockSpec(memory_space=pltpu.SMEM)
params = pltpu.CompilerParams(vmem_limit_bytes=40 * 1024 * 1024)


def call(kernel, out_shape, specs, *operands, name):
    return pl.pallas_call(
        kernel,
        out_shape=out_shape,
        in_specs=specs,
        out_specs=jax.tree.map(lambda _: vmem, out_shape),
        compiler_params=params,
        name=name,
    )(*operands)


def on_device(states, potential, owners):
    count, planes, ny, nx = states.shape
    rows = planes * ny
    doms, bands = lax.axis_size("dom"), lax.axis_size("band")
    weight = 1.0 / float(planes * doms * ny * nx)
    band = lax.axis_index("band")
    inside, beside, along_x = stencil_matrices(planes, ny, nx)
    states = states.reshape(count, rows, nx)
    potential = potential.reshape(rows, nx)
    block = jax.ShapeDtypeStruct(states.shape, bf16)
    wide = jax.ShapeDtypeStruct(states.shape, f32)
    cells = (rows, nx)
    groups = [list(range(start, start + PLANE)) for start in range(0, bands, PLANE)]

    def both_ways(values):
        ring = [(i, (i + 1) % doms) for i in range(doms)]
        return lax.ppermute(values, "dom", ring), lax.ppermute(values, "dom", [(b, a) for a, b in ring])

    def along_z(values, step):
        pairs = []
        for b in range(bands):
            for d in range(doms):
                place = (b // PLANE * doms + d + step) % (bands // PLANE * doms)
                pairs.append((b * doms + d, (place // doms * PLANE + b % PLANE) * doms + place % doms))
        return lax.ppermute(values, ("band", "dom"), pairs)

    hbm = pl.BlockSpec(memory_space=pltpu.HBM)
    twice = pl.pallas_call(
        twice_kernel,
        out_shape=jax.ShapeDtypeStruct((ROUNDS * count,) + cells, bf16),
        in_specs=[hbm],
        out_specs=hbm,
        scratch_shapes=[pltpu.SemaphoreType.DMA((ROUNDS,))],
        compiler_params=params,
        name="twice",
    )(states)
    pieces = lax.all_to_all(twice, "band", 0, 0, axis_index_groups=groups)
    before, after = both_ways(states)
    flat = jax.ShapeDtypeStruct(cells, f32)
    terms = jax.ShapeDtypeStruct((2,) + cells, bf16)
    inner, diagonal, terms = call(
        first_inner_kernel, (wide, flat, terms), [vmem] * 4, states, potential, inside, along_x, name="first_inner"
    )
    owner = jnp.where((band >> 3) & 1 == 0, owners[0], owners[1])
    mine = lax.dynamic_index_in_dim(pieces, owner & (PLANE - 1), 0, keepdims=False)
    mine = jnp.where(owner >> 4 == band >> 4, mine, jnp.zeros_like(mine))
    other = lax.ppermute(mine, "band", [(i, (i + PLANE) % bands) for i in range(bands)])
    first = call(first_kernel, block, [vmem] * 4, before, after, inner, beside, name="first")
    other, first, terms = lax.optimization_barrier((other, first, terms))
    raw = mine + other
    bundle = jnp.concatenate([raw[None], terms], axis=0)
    before, after = both_ways(first)
    inner = call(second_inner_kernel, wide, [vmem] * 4, first, diagonal, inside, along_x, name="second_inner")
    near_before, near_after = along_z(bundle, 1), along_z(bundle, -1)
    next_before, next_after = along_z(raw, 2), along_z(raw, -2)
    next_after, inner = lax.optimization_barrier((next_after, inner))

    resident = call(second_kernel, block, [vmem] * 5, before, after, inner, states, beside, name="second")

    copies = call(
        owner_kernel, jax.ShapeDtypeStruct((PLANE,) + cells, bf16), [vmem] * 9,
        next_before, near_before, raw, near_after, next_after, diagonal, inside, beside, along_x, name="owner",
    )
    gathered = lax.all_to_all(copies, "band", 0, 0, axis_index_groups=groups)
    gram, owned = call(
        gram_kernel,
        (
            jax.ShapeDtypeStruct((ROUNDS * count, ROUNDS * count * GROUP), f32),
            jax.ShapeDtypeStruct((ROUNDS * count * GROUP, rows // GROUP * nx), bf16),
        ),
        [vmem] * 2, gathered, resident, name="gram",
    )
    gram = gram + lax.ppermute(gram, "dom", [(i, i ^ 1) for i in range(doms)])
    gram = gram + sum(lax.ppermute(gram, "dom", [(i, i ^ s) for i in range(doms)]) for s in range(2, doms, 2))
    result = call(
        functools.partial(project_kernel, weight), block, [vmem] * 3, gram, owned, resident, name="project"
    )
    return result.reshape(count, planes, ny, nx)


def solution(mesh):
    return jax.shard_map(
        on_device,
        mesh=mesh,
        in_specs=(P("band", "dom", None, None), P("dom", None, None), P()),
        out_specs=P("band", "dom", None, None),
        check_vma=False,
    )
```

```python
import functools

import jax
import jax.numpy as jnp
import numpy as np
from jax import lax
from jax.experimental import pallas as pl
from jax.experimental.pallas import tpu as pltpu
from jax.sharding import PartitionSpec as P

ROUNDS = 2
PLANE = 16
GROUP = 8

stencil_weights = (
    -5369.0 / 1800.0,
    12.0 / 7.0,
    -15.0 / 56.0,
    10.0 / 189.0,
    -1.0 / 112.0,
    2.0 / 1925.0,
    -1.0 / 16632.0,
)
filter_center = 6.0
filter_halfwidth = 5.0
bf16 = jnp.bfloat16
f32 = jnp.float32


def halves(matrix):
    matrix = matrix.astype(np.float32)
    high = matrix.astype(bf16)
    low = (matrix - high.astype(np.float32)).astype(bf16)
    return high, low


def stencil_matrices(planes, ny, nx):
    scale = -0.5 / filter_halfwidth
    rows = planes * ny
    left = np.zeros((rows, 3 * rows), np.float64)
    for p in range(planes):
        for y in range(ny):
            for k in range(1, 7):
                for sign in (k, -k):
                    left[p * ny + y, (planes + p + sign) * ny + y] += scale * stencil_weights[k]
                    left[p * ny + y, (planes + p) * ny + (y + sign) % ny] += scale * stencil_weights[k]
    along_x = np.zeros((nx, nx), np.float64)
    for x in range(nx):
        for k in range(1, 7):
            for sign in (k, -k):
                along_x[(x + sign) % nx, x] += scale * stencil_weights[k]
    inside = np.concatenate(halves(left[:, rows : 2 * rows]), axis=0)
    beside = np.concatenate(halves(np.concatenate([left[:, :rows], left[:, 2 * rows :]], axis=1)), axis=0)
    return tuple(jnp.asarray(m) for m in (inside, beside, np.concatenate(halves(along_x), axis=1)))


def diagonal_of(potential):
    return (-1.5 * stencil_weights[0] - filter_center) / filter_halfwidth + potential * (1.0 / filter_halfwidth)


def inner_part(center, diagonals, inside, along_x):
    count, rows, nx = center.shape
    zy = jnp.dot(inside, jnp.concatenate([center[s] for s in range(count)], axis=1), preferred_element_type=f32)
    zy = zy[:rows] + zy[rows:]
    x = jnp.dot(center.reshape(count * rows, nx), along_x, preferred_element_type=f32)
    x = (x[:, :nx] + x[:, nx:]).reshape(count, rows, nx)
    return [zy[:, s * nx : (s + 1) * nx] + x[s] + diagonals[s] * center[s].astype(f32) for s in range(count)]


def outer_part(before, after, beside):
    count, rows, nx = before.shape
    slabs = [jnp.concatenate([before[s], after[s]], axis=0) for s in range(count)]
    zy = jnp.dot(beside, jnp.concatenate(slabs, axis=1), preferred_element_type=f32)
    zy = zy[:rows] + zy[rows:]
    return [zy[:, s * nx : (s + 1) * nx] for s in range(count)]


def first_inner_kernel(center, potential, inside, along_x, out, diagonal_out, terms_out):
    diagonal = diagonal_of(potential[...])
    diagonal_out[...] = diagonal
    high = potential[...].astype(bf16)
    terms_out[0] = high
    terms_out[1] = (potential[...] - high.astype(f32)).astype(bf16)
    for s, value in enumerate(inner_part(center[...], [diagonal] * center.shape[0], inside[...], along_x[...])):
        out[s] = value


def second_inner_kernel(center, diagonal, inside, along_x, out):
    for s, value in enumerate(inner_part(center[...], [diagonal[...]] * center.shape[0], inside[...], along_x[...])):
        out[s] = value


def first_kernel(after, before, inner, beside, out):
    for s, value in enumerate(outer_part(before[...], after[...], beside[...])):
        out[s] = (inner[s] + value).astype(bf16)


def second_kernel(after, before, inner, states, beside, out):
    for s, value in enumerate(outer_part(before[...], after[...], beside[...])):
        out[s] = (2.0 * (inner[s] + value) - states[s].astype(f32)).astype(bf16)


def owner_kernel(near_d, near_b, slab_e, slab_a, slab_c, diagonal, inside, beside, along_x, out):
    inside, beside, along_x = inside[...], beside[...], along_x[...]
    middle = jnp.stack([near_b[0], slab_c[...], near_d[0]])
    before = jnp.stack([slab_a[...], near_b[0], slab_c[...]])
    after = jnp.stack([slab_c[...], near_d[0], slab_e[...]])
    outer = outer_part(before, after, beside)
    beside_diagonals = [diagonal_of(n[1].astype(f32) + n[2].astype(f32)) for n in (near_b, near_d)]
    diagonals = [beside_diagonals[0], diagonal[...], beside_diagonals[1]]
    inner = inner_part(middle, diagonals, inside, along_x)
    first = [(i + o).astype(bf16)[None] for i, o in zip(inner, outer)]
    value = inner_part(first[1], diagonals[1:2], inside, along_x)[0] + outer_part(first[0], first[2], beside)[0]
    block = (2.0 * value - slab_c[...].astype(f32)).astype(bf16)
    for target in range(PLANE):
        out[target] = block


def by_rows(blocks):
    return jnp.concatenate(
        [jnp.concatenate([b[r : r + GROUP] for r in range(0, b.shape[0], GROUP)], axis=1) for b in blocks], axis=0
    ).astype(bf16)


def same_row(shape):
    row = lax.broadcasted_iota(jnp.int32, shape, 0) % GROUP
    return row == lax.broadcasted_iota(jnp.int32, shape, 1) % GROUP


def gram_kernel(gathered, resident, out, rows_out):
    count = resident.shape[0]
    blocks = []
    for turn in range(ROUNDS):
        for s in range(count):
            blocks.append(gathered[(2 * (s // 4) + turn) * 4 + s % 4].astype(f32))
    owned = by_rows(blocks)
    against = jnp.concatenate(
        [by_rows([resident[j].astype(f32) for j in range(count)]), owned[: count * GROUP]], axis=0
    )
    products = lax.dot_general(owned, against, (((1,), (1,)), ((), ())), preferred_element_type=f32)
    products = jnp.where(same_row(products.shape), products, 0.0)
    out[...] = jnp.sum(products.reshape(ROUNDS * count, GROUP, products.shape[1]), axis=1)
    rows_out[...] = owned


def project_kernel(weight, gram, owned, resident, out):
    count, rows, nx = resident.shape
    lanes = gram.shape[1]
    group = lax.broadcasted_iota(jnp.int32, (lanes, lanes), 0) // GROUP
    same_group = jnp.where(group == lax.broadcasted_iota(jnp.int32, (lanes, lanes), 1) // GROUP, 1.0, 0.0)
    left, terms = gram[...], []
    for _ in range(3):
        terms.append(left.astype(bf16))
        left = left - terms[-1].astype(f32)
    sums = jnp.dot(jnp.concatenate(terms, axis=0), same_group.astype(bf16), preferred_element_type=f32)
    sums = sums[: 2 * count] + (sums[2 * count : 4 * count] + sums[4 * count :])
    one = sums[:count] * weight
    two = sums[count:]
    for k in range(count):
        lane = (count + k) * GROUP
        two = two - sums[count:, lane : lane + 1] * one[k : k + 1]
    coef = jnp.concatenate([one, two * weight], axis=0)
    spread = jnp.broadcast_to(coef[:, None, :], (ROUNDS * count, GROUP, lanes)).reshape(lanes, lanes)
    spread = jnp.where(same_row(spread.shape), spread, 0.0).T[: count * GROUP]
    high = spread.astype(bf16)
    low = (spread - high.astype(f32)).astype(bf16)
    taken = jnp.dot(jnp.concatenate([high, low], axis=0), owned[...], preferred_element_type=f32)
    taken = taken[: count * GROUP] + taken[count * GROUP :]
    for j in range(count):
        mine = taken[j * GROUP : (j + 1) * GROUP]
        mine = jnp.concatenate([mine[:, b * nx : (b + 1) * nx] for b in range(rows // GROUP)], axis=0)
        out[j] = (resident[j].astype(f32) - mine).astype(bf16)


vmem = pl.BlockSpec(memory_space=pltpu.VMEM)
smem = pl.BlockSpec(memory_space=pltpu.SMEM)
params = pltpu.CompilerParams(vmem_limit_bytes=40 * 1024 * 1024)


def call(kernel, out_shape, specs, *operands, name, cost=None):
    return pl.pallas_call(
        kernel,
        out_shape=out_shape,
        in_specs=specs,
        out_specs=jax.tree.map(lambda _: vmem, out_shape),
        compiler_params=params,
        cost_estimate=cost and pl.CostEstimate(flops=cost, bytes_accessed=1 << 20, transcendentals=0),
        name=name,
    )(*operands)


def on_device(states, potential, owners):
    count, planes, ny, nx = states.shape
    rows = planes * ny
    doms, bands = lax.axis_size("dom"), lax.axis_size("band")
    weight = 1.0 / float(planes * doms * ny * nx)
    band = lax.axis_index("band")
    inside, beside, along_x = stencil_matrices(planes, ny, nx)
    states = states.reshape(count, rows, nx)
    potential = potential.reshape(rows, nx)
    block = jax.ShapeDtypeStruct(states.shape, bf16)
    wide = jax.ShapeDtypeStruct(states.shape, f32)
    cells = (rows, nx)
    groups = [list(range(start, start + PLANE)) for start in range(0, bands, PLANE)]

    def both_ways(values):
        ring = [(i, (i + 1) % doms) for i in range(doms)]
        return lax.ppermute(values, "dom", ring), lax.ppermute(values, "dom", [(b, a) for a, b in ring])

    def along_z(values, step):
        pairs = []
        for b in range(bands):
            for d in range(doms):
                place = (b // PLANE * doms + d + step) % (bands // PLANE * doms)
                pairs.append((b * doms + d, (place // doms * PLANE + b % PLANE) * doms + place % doms))
        return lax.ppermute(values, ("band", "dom"), pairs)

    x_odd, z_hi = (band >> 2) & 1, band >> 4
    spread_groups = [
        [z * PLANE + x * 4 + y for x in (odd, odd + 2) for y in range(4)] for z in range(2) for odd in range(2)
    ]
    pieces = lax.all_to_all(states, "band", 0, 0, axis_index_groups=spread_groups)
    before, after = both_ways(states)
    flat = jax.ShapeDtypeStruct(cells, f32)
    terms = jax.ShapeDtypeStruct((2,) + cells, bf16)
    inner, diagonal, terms = call(
        first_inner_kernel, (wide, flat, terms), [vmem] * 4, states, potential, inside, along_x, name="first_inner"
    )
    def piece_of(owner):
        piece = lax.dynamic_index_in_dim(pieces, ((owner >> 3) & 1) * 4 + (owner & 3), 0, keepdims=False)
        here = jnp.logical_and(owner >> 4 == z_hi, (owner >> 2) & 1 == x_odd)
        return jnp.where(here, piece, jnp.zeros_like(piece))

    kept = piece_of(jnp.where(x_odd == 0, owners[0], owners[1]))
    sent = piece_of(jnp.where(x_odd == 0, owners[1], owners[0]))
    mine = kept + lax.ppermute(sent, "band", [(i, i ^ 4) for i in range(bands)])
    other = lax.ppermute(mine, "band", [(i, i ^ PLANE) for i in range(bands)])
    first = call(first_kernel, block, [vmem] * 4, after, before, inner, beside, name="first", cost=2*10**10)
    other, first, terms = lax.optimization_barrier((other, first, terms))
    raw = mine + other
    bundle = jnp.concatenate([raw[None], terms], axis=0)
    before, after = both_ways(first)
    inner = call(second_inner_kernel, wide, [vmem] * 4, first, diagonal, inside, along_x, name="second_inner", cost=None)
    near_before, near_after = along_z(bundle, 1), along_z(bundle, -1)
    next_before, next_after = along_z(raw, 2), along_z(raw, -2)
    next_after, inner = lax.optimization_barrier((next_after, inner))

    resident = call(second_kernel, block, [vmem] * 5, after, before, inner, states, beside, name="second")

    copies = call(
        owner_kernel, jax.ShapeDtypeStruct((PLANE,) + cells, bf16), [vmem] * 9,
        near_after, near_before, next_after, next_before, raw, diagonal, inside, beside, along_x, name="owner",
    )
    gathered = lax.all_to_all(copies, "band", 0, 0, axis_index_groups=groups)
    gram, owned = call(
        gram_kernel,
        (
            jax.ShapeDtypeStruct((ROUNDS * count, ROUNDS * count * GROUP), f32),
            jax.ShapeDtypeStruct((ROUNDS * count * GROUP, rows // GROUP * nx), bf16),
        ),
        [vmem] * 2, gathered, resident, name="gram",
    )
    gram = gram + lax.ppermute(gram, "dom", [(i, i ^ 1) for i in range(doms)])
    gram = gram + sum(lax.ppermute(gram, "dom", [(i, i ^ s) for i in range(doms)]) for s in range(doms - 2, 0, -2))
    result = call(
        functools.partial(project_kernel, weight), block, [vmem] * 3, gram, owned, resident, name="project"
    )
    return result.reshape(count, planes, ny, nx)


def solution(mesh):
    return jax.shard_map(
        on_device,
        mesh=mesh,
        in_specs=(P("band", "dom", None, None), P("dom", None, None), P()),
        out_specs=P("band", "dom", None, None),
        check_vma=False,
    )
```

```python
import functools

import jax
import jax.numpy as jnp
import numpy as np
from jax import lax
from jax.experimental import pallas as pl
from jax.experimental.pallas import tpu as pltpu
from jax.sharding import PartitionSpec as P

ROUNDS = 2
PLANE = 16
GROUP = 8

stencil_weights = (
    -5369.0 / 1800.0,
    12.0 / 7.0,
    -15.0 / 56.0,
    10.0 / 189.0,
    -1.0 / 112.0,
    2.0 / 1925.0,
    -1.0 / 16632.0,
)
filter_center = 6.0
filter_halfwidth = 5.0
bf16 = jnp.bfloat16
f32 = jnp.float32


def halves(matrix):
    matrix = matrix.astype(np.float32)
    high = matrix.astype(bf16)
    low = (matrix - high.astype(np.float32)).astype(bf16)
    return high, low


def stencil_matrices(planes, ny, nx):
    scale = -0.5 / filter_halfwidth
    rows = planes * ny
    left = np.zeros((rows, 3 * rows), np.float64)
    for p in range(planes):
        for y in range(ny):
            for k in range(1, 7):
                for sign in (k, -k):
                    left[p * ny + y, (planes + p + sign) * ny + y] += scale * stencil_weights[k]
                    left[p * ny + y, (planes + p) * ny + (y + sign) % ny] += scale * stencil_weights[k]
    along_x = np.zeros((nx, nx), np.float64)
    for x in range(nx):
        for k in range(1, 7):
            for sign in (k, -k):
                along_x[(x + sign) % nx, x] += scale * stencil_weights[k]
    inside = np.concatenate(halves(left[:, rows : 2 * rows]), axis=0)
    beside = np.concatenate(halves(np.concatenate([left[:, :rows], left[:, 2 * rows :]], axis=1)), axis=0)
    return tuple(jnp.asarray(m) for m in (inside, beside, np.concatenate(halves(along_x), axis=1)))


def diagonal_of(potential):
    return (-1.5 * stencil_weights[0] - filter_center) / filter_halfwidth + potential * (1.0 / filter_halfwidth)


def inner_part(center, diagonals, inside, along_x):
    count, rows, nx = center.shape
    zy = jnp.dot(inside, jnp.concatenate([center[s] for s in range(count)], axis=1), preferred_element_type=f32)
    zy = zy[:rows] + zy[rows:]
    x = jnp.dot(center.reshape(count * rows, nx), along_x, preferred_element_type=f32)
    x = (x[:, :nx] + x[:, nx:]).reshape(count, rows, nx)
    return [zy[:, s * nx : (s + 1) * nx] + x[s] + diagonals[s] * center[s].astype(f32) for s in range(count)]


def outer_part(before, after, beside):
    count, rows, nx = before.shape
    slabs = [jnp.concatenate([before[s], after[s]], axis=0) for s in range(count)]
    zy = jnp.dot(beside, jnp.concatenate(slabs, axis=1), preferred_element_type=f32)
    zy = zy[:rows] + zy[rows:]
    return [zy[:, s * nx : (s + 1) * nx] for s in range(count)]


def first_inner_kernel(center, potential, inside, along_x, out, diagonal_out, terms_out):
    diagonal = diagonal_of(potential[...])
    diagonal_out[...] = diagonal
    high = potential[...].astype(bf16)
    terms_out[0] = high
    terms_out[1] = (potential[...] - high.astype(f32)).astype(bf16)
    for s, value in enumerate(inner_part(center[...], [diagonal] * center.shape[0], inside[...], along_x[...])):
        out[s] = value


def second_inner_kernel(center, diagonal, inside, along_x, out):
    for s, value in enumerate(inner_part(center[...], [diagonal[...]] * center.shape[0], inside[...], along_x[...])):
        out[s] = value


def first_kernel(after, before, inner, beside, out):
    for s, value in enumerate(outer_part(before[...], after[...], beside[...])):
        out[s] = (inner[s] + value).astype(bf16)


def second_kernel(after, before, inner, states, beside, out):
    for s, value in enumerate(outer_part(before[...], after[...], beside[...])):
        out[s] = (2.0 * (inner[s] + value) - states[s].astype(f32)).astype(bf16)


def owner_kernel(near_d, near_b, slab_e, slab_a, slab_c, diagonal, inside, beside, along_x, out):
    inside, beside, along_x = inside[...], beside[...], along_x[...]
    middle = jnp.stack([near_b[0], slab_c[...], near_d[0]])
    before = jnp.stack([slab_a[...], near_b[0], slab_c[...]])
    after = jnp.stack([slab_c[...], near_d[0], slab_e[...]])
    outer = outer_part(before, after, beside)
    beside_diagonals = [diagonal_of(n[1].astype(f32) + n[2].astype(f32)) for n in (near_b, near_d)]
    diagonals = [beside_diagonals[0], diagonal[...], beside_diagonals[1]]
    inner = inner_part(middle, diagonals, inside, along_x)
    first = [(i + o).astype(bf16)[None] for i, o in zip(inner, outer)]
    value = inner_part(first[1], diagonals[1:2], inside, along_x)[0] + outer_part(first[0], first[2], beside)[0]
    block = (2.0 * value - slab_c[...].astype(f32)).astype(bf16)
    for target in range(PLANE):
        out[target] = block


def by_rows(blocks):
    return jnp.concatenate(
        [jnp.concatenate([b[r : r + GROUP] for r in range(0, b.shape[0], GROUP)], axis=1) for b in blocks], axis=0
    ).astype(bf16)


def same_row(shape):
    row = lax.broadcasted_iota(jnp.int32, shape, 0) % GROUP
    return row == lax.broadcasted_iota(jnp.int32, shape, 1) % GROUP


def gram_kernel(gathered, resident, out, rows_out):
    count = resident.shape[0]
    blocks = []
    for turn in range(ROUNDS):
        for s in range(count):
            blocks.append(gathered[(2 * (s // 4) + turn) * 4 + s % 4].astype(f32))
    owned = by_rows(blocks)
    against = jnp.concatenate(
        [by_rows([resident[j].astype(f32) for j in range(count)]), owned[: count * GROUP]], axis=0
    )
    products = lax.dot_general(owned, against, (((1,), (1,)), ((), ())), preferred_element_type=f32)
    products = jnp.where(same_row(products.shape), products, 0.0)
    out[...] = jnp.sum(products.reshape(ROUNDS * count, GROUP, products.shape[1]), axis=1)
    rows_out[...] = owned


def project_kernel(weight, part_a, part_b, part_c, gram, owned, resident, out):
    count, rows, nx = resident.shape
    lanes = gram.shape[1]
    group = lax.broadcasted_iota(jnp.int32, (lanes, lanes), 0) // GROUP
    same_group = jnp.where(group == lax.broadcasted_iota(jnp.int32, (lanes, lanes), 1) // GROUP, 1.0, 0.0)
    left, terms = (gram[...] + part_a[...]) + (part_b[...] + part_c[...]), []
    for _ in range(3):
        terms.append(left.astype(bf16))
        left = left - terms[-1].astype(f32)
    sums = jnp.dot(jnp.concatenate(terms, axis=0), same_group.astype(bf16), preferred_element_type=f32)
    sums = sums[: 2 * count] + (sums[2 * count : 4 * count] + sums[4 * count :])
    one = sums[:count] * weight
    two = sums[count:]
    for k in range(count):
        lane = (count + k) * GROUP
        two = two - sums[count:, lane : lane + 1] * one[k : k + 1]
    coef = jnp.concatenate([one, two * weight], axis=0)
    spread = jnp.broadcast_to(coef[:, None, :], (ROUNDS * count, GROUP, lanes)).reshape(lanes, lanes)
    spread = jnp.where(same_row(spread.shape), spread, 0.0).T[: count * GROUP]
    high = spread.astype(bf16)
    low = (spread - high.astype(f32)).astype(bf16)
    taken = jnp.dot(jnp.concatenate([high, low], axis=0), owned[...], preferred_element_type=f32)
    taken = taken[: count * GROUP] + taken[count * GROUP :]
    for j in range(count):
        mine = taken[j * GROUP : (j + 1) * GROUP]
        mine = jnp.concatenate([mine[:, b * nx : (b + 1) * nx] for b in range(rows // GROUP)], axis=0)
        out[j] = (resident[j].astype(f32) - mine).astype(bf16)


vmem = pl.BlockSpec(memory_space=pltpu.VMEM)
smem = pl.BlockSpec(memory_space=pltpu.SMEM)
params = pltpu.CompilerParams(vmem_limit_bytes=40 * 1024 * 1024)


def call(kernel, out_shape, specs, *operands, name, cost=None):
    return pl.pallas_call(
        kernel,
        out_shape=out_shape,
        in_specs=specs,
        out_specs=jax.tree.map(lambda _: vmem, out_shape),
        compiler_params=params,
        cost_estimate=cost and pl.CostEstimate(flops=cost, bytes_accessed=1 << 20, transcendentals=0),
        name=name,
    )(*operands)


def on_device(states, potential, owners):
    count, planes, ny, nx = states.shape
    rows = planes * ny
    doms, bands = lax.axis_size("dom"), lax.axis_size("band")
    weight = 1.0 / float(planes * doms * ny * nx)
    band = lax.axis_index("band")
    inside, beside, along_x = stencil_matrices(planes, ny, nx)
    states = states.reshape(count, rows, nx)
    potential = potential.reshape(rows, nx)
    block = jax.ShapeDtypeStruct(states.shape, bf16)
    wide = jax.ShapeDtypeStruct(states.shape, f32)
    cells = (rows, nx)
    groups = [list(range(start, start + PLANE)) for start in range(0, bands, PLANE)]

    def both_ways(values):
        ring = [(i, (i + 1) % doms) for i in range(doms)]
        return lax.ppermute(values, "dom", ring), lax.ppermute(values, "dom", [(b, a) for a, b in ring])

    def along_z(values, step):
        pairs = []
        for b in range(bands):
            for d in range(doms):
                place = (b // PLANE * doms + d + step) % (bands // PLANE * doms)
                pairs.append((b * doms + d, (place // doms * PLANE + b % PLANE) * doms + place % doms))
        return lax.ppermute(values, ("band", "dom"), pairs)

    x_odd, z_hi = (band >> 2) & 1, band >> 4
    spread_groups = [
        [z * PLANE + x * 4 + y for x in (odd, odd + 2) for y in range(4)] for z in range(2) for odd in range(2)
    ]
    pieces = lax.all_to_all(states, "band", 0, 0, axis_index_groups=spread_groups)
    before, after = both_ways(states)
    flat = jax.ShapeDtypeStruct(cells, f32)
    terms = jax.ShapeDtypeStruct((2,) + cells, bf16)
    inner, diagonal, terms = call(
        first_inner_kernel, (wide, flat, terms), [vmem] * 4, states, potential, inside, along_x, name="first_inner"
    )
    def piece_of(owner):
        piece = lax.dynamic_index_in_dim(pieces, ((owner >> 3) & 1) * 4 + (owner & 3), 0, keepdims=False)
        here = jnp.logical_and(owner >> 4 == z_hi, (owner >> 2) & 1 == x_odd)
        return jnp.where(here, piece, jnp.zeros_like(piece))

    kept = piece_of(jnp.where(x_odd == 0, owners[0], owners[1]))
    sent = piece_of(jnp.where(x_odd == 0, owners[1], owners[0]))
    mine = kept + lax.ppermute(sent, "band", [(i, i ^ 4) for i in range(bands)])
    other = lax.ppermute(mine, "band", [(i, i ^ PLANE) for i in range(bands)])
    first = call(first_kernel, block, [vmem] * 4, after, before, inner, beside, name="first", cost=2*10**10)
    other, first, terms = lax.optimization_barrier((other, first, terms))
    raw = mine + other
    bundle = jnp.concatenate([raw[None], terms], axis=0)
    before, after = both_ways(first)
    inner = call(second_inner_kernel, wide, [vmem] * 4, first, diagonal, inside, along_x, name="second_inner", cost=None)
    near_before, near_after = along_z(bundle, 1), along_z(bundle, -1)
    next_before, next_after = along_z(raw, 2), along_z(raw, -2)
    next_after, inner = lax.optimization_barrier((next_after, inner))

    resident = call(second_kernel, block, [vmem] * 5, after, before, inner, states, beside, name="second")

    copies = call(
        owner_kernel, jax.ShapeDtypeStruct((PLANE,) + cells, bf16), [vmem] * 9,
        near_after, near_before, next_after, next_before, raw, diagonal, inside, beside, along_x, name="owner",
    )
    gathered = lax.all_to_all(copies, "band", 0, 0, axis_index_groups=groups)
    gram, owned = call(
        gram_kernel,
        (
            jax.ShapeDtypeStruct((ROUNDS * count, ROUNDS * count * GROUP), f32),
            jax.ShapeDtypeStruct((ROUNDS * count * GROUP, rows // GROUP * nx), bf16),
        ),
        [vmem] * 2, gathered, resident, name="gram",
    )
    gram = gram + lax.ppermute(gram, "dom", [(i, i ^ 1) for i in range(doms)])
    parts = [lax.ppermute(gram, "dom", [(i, i ^ s) for i in range(doms)]) for s in (6, 2, 4)]
    result = call(
        functools.partial(project_kernel, weight), block, [vmem] * 6, *parts, gram, owned, resident, name="project"
    )
    return result.reshape(count, planes, ny, nx)


def solution(mesh):
    return jax.shard_map(
        on_device,
        mesh=mesh,
        in_specs=(P("band", "dom", None, None), P("dom", None, None), P()),
        out_specs=P("band", "dom", None, None),
        check_vma=False,
    )
```

```python
import functools

import jax
import jax.numpy as jnp
import numpy as np
from jax import lax
from jax.experimental import pallas as pl
from jax.experimental.pallas import tpu as pltpu
from jax.sharding import PartitionSpec as P

ROUNDS = 2
PLANE = 16
GROUP = 8

stencil_weights = (
    -5369.0 / 1800.0,
    12.0 / 7.0,
    -15.0 / 56.0,
    10.0 / 189.0,
    -1.0 / 112.0,
    2.0 / 1925.0,
    -1.0 / 16632.0,
)
filter_center = 6.0
filter_halfwidth = 5.0
bf16 = jnp.bfloat16
f32 = jnp.float32


def halves(matrix):
    matrix = matrix.astype(np.float32)
    high = matrix.astype(bf16)
    low = (matrix - high.astype(np.float32)).astype(bf16)
    return high, low


def stencil_matrices(planes, ny, nx):
    scale = -0.5 / filter_halfwidth
    rows = planes * ny
    left = np.zeros((rows, 3 * rows), np.float64)
    for p in range(planes):
        for y in range(ny):
            for k in range(1, 7):
                for sign in (k, -k):
                    left[p * ny + y, (planes + p + sign) * ny + y] += scale * stencil_weights[k]
                    left[p * ny + y, (planes + p) * ny + (y + sign) % ny] += scale * stencil_weights[k]
    along_x = np.zeros((nx, nx), np.float64)
    for x in range(nx):
        for k in range(1, 7):
            for sign in (k, -k):
                along_x[(x + sign) % nx, x] += scale * stencil_weights[k]
    inside = np.concatenate(halves(left[:, rows : 2 * rows]), axis=0)
    beside = np.concatenate(halves(np.concatenate([left[:, :rows], left[:, 2 * rows :]], axis=1)), axis=0)
    return tuple(jnp.asarray(m) for m in (inside, beside, np.concatenate(halves(along_x), axis=1)))


def diagonal_of(potential):
    return (-1.5 * stencil_weights[0] - filter_center) / filter_halfwidth + potential * (1.0 / filter_halfwidth)


def inner_part(center, diagonals, inside, along_x):
    count, rows, nx = center.shape
    zy = jnp.dot(inside, jnp.concatenate([center[s] for s in range(count)], axis=1), preferred_element_type=f32)
    zy = zy[:rows] + zy[rows:]
    x = jnp.dot(center.reshape(count * rows, nx), along_x, preferred_element_type=f32)
    x = (x[:, :nx] + x[:, nx:]).reshape(count, rows, nx)
    return [zy[:, s * nx : (s + 1) * nx] + x[s] + diagonals[s] * center[s].astype(f32) for s in range(count)]


def outer_part(before, after, beside):
    count, rows, nx = before.shape
    slabs = [jnp.concatenate([before[s], after[s]], axis=0) for s in range(count)]
    zy = jnp.dot(beside, jnp.concatenate(slabs, axis=1), preferred_element_type=f32)
    zy = zy[:rows] + zy[rows:]
    return [zy[:, s * nx : (s + 1) * nx] for s in range(count)]


def first_inner_kernel(center, potential, inside, along_x, out, diagonal_out, terms_out):
    diagonal = diagonal_of(potential[...])
    diagonal_out[...] = diagonal
    high = potential[...].astype(bf16)
    terms_out[0] = high
    terms_out[1] = (potential[...] - high.astype(f32)).astype(bf16)
    for s, value in enumerate(inner_part(center[...], [diagonal] * center.shape[0], inside[...], along_x[...])):
        out[s] = value


def second_inner_kernel(center, diagonal, inside, along_x, out):
    for s, value in enumerate(inner_part(center[...], [diagonal[...]] * center.shape[0], inside[...], along_x[...])):
        out[s] = value


def first_kernel(after, before, inner, beside, out):
    for s, value in enumerate(outer_part(before[...], after[...], beside[...])):
        out[s] = (inner[s] + value).astype(bf16)


def second_kernel(after, before, inner, states, beside, out):
    for s, value in enumerate(outer_part(before[...], after[...], beside[...])):
        out[s] = (2.0 * (inner[s] + value) - states[s].astype(f32)).astype(bf16)


def owner_kernel(near_d, near_b, slab_e, slab_a, slab_c, raw_inner, diagonal, inside, beside, along_x, out):
    inside, beside, along_x = inside[...], beside[...], along_x[...]
    middle = jnp.stack([near_b[0], near_d[0]])
    before = jnp.stack([slab_a[...], near_b[0], slab_c[...]])
    after = jnp.stack([slab_c[...], near_d[0], slab_e[...]])
    outer = outer_part(before, after, beside)
    beside_diagonals = [diagonal_of(n[1].astype(f32) + n[2].astype(f32)) for n in (near_b, near_d)]
    inner = inner_part(middle, beside_diagonals, inside, along_x)
    inner = [inner[0], raw_inner[0], inner[1]]
    first = [(i + o).astype(bf16)[None] for i, o in zip(inner, outer)]
    value = inner_part(first[1], [diagonal[...]], inside, along_x)[0] + outer_part(first[0], first[2], beside)[0]
    block = (2.0 * value - slab_c[...].astype(f32)).astype(bf16)
    for target in range(PLANE):
        out[target] = block


def by_rows(blocks):
    return jnp.concatenate(
        [jnp.concatenate([b[r : r + GROUP] for r in range(0, b.shape[0], GROUP)], axis=1) for b in blocks], axis=0
    ).astype(bf16)


def same_row(shape):
    row = lax.broadcasted_iota(jnp.int32, shape, 0) % GROUP
    return row == lax.broadcasted_iota(jnp.int32, shape, 1) % GROUP


def gram_kernel(gathered, resident, out, rows_out):
    count = resident.shape[0]
    blocks = []
    for turn in range(ROUNDS):
        for s in range(count):
            blocks.append(gathered[(2 * (s // 4) + turn) * 4 + s % 4].astype(f32))
    owned = by_rows(blocks)
    against = jnp.concatenate(
        [by_rows([resident[j].astype(f32) for j in range(count)]), owned[: count * GROUP]], axis=0
    )
    products = lax.dot_general(owned, against, (((1,), (1,)), ((), ())), preferred_element_type=f32)
    products = jnp.where(same_row(products.shape), products, 0.0)
    out[...] = jnp.sum(products.reshape(ROUNDS * count, GROUP, products.shape[1]), axis=1)
    rows_out[...] = owned


def project_kernel(weight, part_a, part_b, part_c, gram, owned, resident, out):
    count, rows, nx = resident.shape
    lanes = gram.shape[1]
    group = lax.broadcasted_iota(jnp.int32, (lanes, lanes), 0) // GROUP
    same_group = jnp.where(group == lax.broadcasted_iota(jnp.int32, (lanes, lanes), 1) // GROUP, 1.0, 0.0)
    left, terms = (gram[...] + part_a[...]) + (part_b[...] + part_c[...]), []
    for _ in range(3):
        terms.append(left.astype(bf16))
        left = left - terms[-1].astype(f32)
    sums = jnp.dot(jnp.concatenate(terms, axis=0), same_group.astype(bf16), preferred_element_type=f32)
    sums = sums[: 2 * count] + (sums[2 * count : 4 * count] + sums[4 * count :])
    one = sums[:count] * weight
    two = sums[count:]
    for k in range(count):
        lane = (count + k) * GROUP
        two = two - sums[count:, lane : lane + 1] * one[k : k + 1]
    coef = jnp.concatenate([one, two * weight], axis=0)
    spread = jnp.broadcast_to(coef[:, None, :], (ROUNDS * count, GROUP, lanes)).reshape(lanes, lanes)
    spread = jnp.where(same_row(spread.shape), spread, 0.0).T[: count * GROUP]
    high = spread.astype(bf16)
    low = (spread - high.astype(f32)).astype(bf16)
    taken = jnp.dot(jnp.concatenate([high, low], axis=0), owned[...], preferred_element_type=f32)
    taken = taken[: count * GROUP] + taken[count * GROUP :]
    for j in range(count):
        mine = taken[j * GROUP : (j + 1) * GROUP]
        mine = jnp.concatenate([mine[:, b * nx : (b + 1) * nx] for b in range(rows // GROUP)], axis=0)
        out[j] = (resident[j].astype(f32) - mine).astype(bf16)


vmem = pl.BlockSpec(memory_space=pltpu.VMEM)
smem = pl.BlockSpec(memory_space=pltpu.SMEM)
params = pltpu.CompilerParams(vmem_limit_bytes=40 * 1024 * 1024)


def call(kernel, out_shape, specs, *operands, name, cost=None):
    return pl.pallas_call(
        kernel,
        out_shape=out_shape,
        in_specs=specs,
        out_specs=jax.tree.map(lambda _: vmem, out_shape),
        compiler_params=params,
        cost_estimate=cost and pl.CostEstimate(flops=cost, bytes_accessed=1 << 20, transcendentals=0),
        name=name,
    )(*operands)


def on_device(states, potential, owners):
    count, planes, ny, nx = states.shape
    rows = planes * ny
    doms, bands = lax.axis_size("dom"), lax.axis_size("band")
    weight = 1.0 / float(planes * doms * ny * nx)
    band = lax.axis_index("band")
    inside, beside, along_x = stencil_matrices(planes, ny, nx)
    states = states.reshape(count, rows, nx)
    potential = potential.reshape(rows, nx)
    block = jax.ShapeDtypeStruct(states.shape, bf16)
    wide = jax.ShapeDtypeStruct(states.shape, f32)
    cells = (rows, nx)
    groups = [list(range(start, start + PLANE)) for start in range(0, bands, PLANE)]

    def both_ways(values):
        ring = [(i, (i + 1) % doms) for i in range(doms)]
        return lax.ppermute(values, "dom", ring), lax.ppermute(values, "dom", [(b, a) for a, b in ring])

    def along_z(values, step):
        pairs = []
        for b in range(bands):
            for d in range(doms):
                place = (b // PLANE * doms + d + step) % (bands // PLANE * doms)
                pairs.append((b * doms + d, (place // doms * PLANE + b % PLANE) * doms + place % doms))
        return lax.ppermute(values, ("band", "dom"), pairs)

    x_odd, z_hi = (band >> 2) & 1, band >> 4
    spread_groups = [
        [z * PLANE + x * 4 + y for x in (odd, odd + 2) for y in range(4)] for z in range(2) for odd in range(2)
    ]
    pieces = lax.all_to_all(states, "band", 0, 0, axis_index_groups=spread_groups)
    before, after = both_ways(states)
    flat = jax.ShapeDtypeStruct(cells, f32)
    terms = jax.ShapeDtypeStruct((2,) + cells, bf16)
    inner, diagonal, terms = call(
        first_inner_kernel, (wide, flat, terms), [vmem] * 4, states, potential, inside, along_x, name="first_inner"
    )
    def piece_of(owner):
        piece = lax.dynamic_index_in_dim(pieces, ((owner >> 3) & 1) * 4 + (owner & 3), 0, keepdims=False)
        here = jnp.logical_and(owner >> 4 == z_hi, (owner >> 2) & 1 == x_odd)
        return jnp.where(here, piece, jnp.zeros_like(piece))

    kept = piece_of(jnp.where(x_odd == 0, owners[0], owners[1]))
    sent = piece_of(jnp.where(x_odd == 0, owners[1], owners[0]))
    mine = kept + lax.ppermute(sent, "band", [(i, i ^ 4) for i in range(bands)])
    other = lax.ppermute(mine, "band", [(i, i ^ PLANE) for i in range(bands)])
    first = call(first_kernel, block, [vmem] * 4, after, before, inner, beside, name="first", cost=2*10**10)
    other, first, terms = lax.optimization_barrier((other, first, terms))
    raw = mine + other
    bundle = jnp.concatenate([raw[None], terms], axis=0)
    before, after = both_ways(first)
    inner = call(second_inner_kernel, wide, [vmem] * 4, first, diagonal, inside, along_x, name="second_inner", cost=None)
    near_before, near_after = along_z(bundle, 1), along_z(bundle, -1)
    next_before, next_after = along_z(raw, 2), along_z(raw, -2)
    next_after, inner = lax.optimization_barrier((next_after, inner))

    resident = call(second_kernel, block, [vmem] * 5, after, before, inner, states, beside, name="second")

    raw_inner = call(
        second_inner_kernel, jax.ShapeDtypeStruct((1,) + cells, f32), [vmem] * 4, raw[None], diagonal, inside, along_x,
        name="raw_inner",
    )
    copies = call(
        owner_kernel, jax.ShapeDtypeStruct((PLANE,) + cells, bf16), [vmem] * 10,
        near_after, near_before, next_after, next_before, raw, raw_inner, diagonal, inside, beside, along_x, name="owner",
    )
    gathered = lax.all_to_all(copies, "band", 0, 0, axis_index_groups=groups)
    gram, owned = call(
        gram_kernel,
        (
            jax.ShapeDtypeStruct((ROUNDS * count, ROUNDS * count * GROUP), f32),
            jax.ShapeDtypeStruct((ROUNDS * count * GROUP, rows // GROUP * nx), bf16),
        ),
        [vmem] * 2, gathered, resident, name="gram",
    )
    gram = gram + lax.ppermute(gram, "dom", [(i, i ^ 1) for i in range(doms)])
    parts = [lax.ppermute(gram, "dom", [(i, i ^ s) for i in range(doms)]) for s in (6, 2, 4)]
    result = call(
        functools.partial(project_kernel, weight), block, [vmem] * 6, *parts, gram, owned, resident, name="project"
    )
    return result.reshape(count, planes, ny, nx)


def solution(mesh):
    return jax.shard_map(
        on_device,
        mesh=mesh,
        in_specs=(P("band", "dom", None, None), P("dom", None, None), P()),
        out_specs=P("band", "dom", None, None),
        check_vma=False,
    )
```
